256 devices in a mesh: path: 16 (over z, core), col: 16 (over y, x).
Axes of the slice: x: 4, y: 4, z: 8, core: 2. Of those that a mesh axis runs over, the one named last changes fastest.
Arguments:
- exposure: bfloat16 [65536, 16384], P('path', 'col'), may hold values from -127 to 127
- scales: float32 [128, 65536], P('col', 'path'), may hold values from 0.003 to 0.27, as said below
- sketch: bfloat16 [32, 16384], P(None, 'col'), may hold values from -0.046875 to 0.046875
Outputs:
- basis: float32 [32, 65536], P(None, 'path')
- projected: float32 [32, 16384], P(None, 'col')
The draws below stay inside these ranges and needn't reach their ends.
Inputs may be any that keep to these rules, and one draw needn't show every extreme that they name: `scales`: positive.
All inputs are finite; a program needn't handle non-finite values.
Results may differ from the reference program's by a relative error of at most 0.0003.
Values sent between devices are 32-bit elements; how exact they have to be, the bound alone decides.
No kernel may reach another device: no remote copies, remote signals or barrier semaphores. Data moves between devices by JAX's collectives and lax.ppermute only.
A program may use at most 64 MiB of HBM per device.

```python
import jax
import jax.numpy as jnp
from jax import lax

PATH_DEV = 4096
SKETCH = 32
PATHS = 65536
COLS = 16384
BLOCKS = 128
N_PATH = 16


def draw_scales(key, part):
    key = jax.random.fold_in(key, 7)
    level = jax.random.uniform(key, (BLOCKS, PATHS), jnp.float32, jnp.log(0.003), jnp.log(0.03))
    ramp = 1.0 + 2.0 * jnp.arange(PATHS, dtype=jnp.float32)[None, :] / PATHS
    value = jnp.exp(level) * ramp
    return value


def block_levels(own_key, dims, split, low, largest):
    def one(axis_at, blocks):
        heights = jax.random.uniform(jax.random.fold_in(jax.random.fold_in(own_key, 6), axis_at), (blocks,), jnp.float32, low / len(split), largest / len(split))
        return jnp.repeat(jnp.exp(heights), dims[axis_at] // blocks).reshape((-1,) + (1,) * (len(dims) - axis_at - 1))

    gain = one(*split[0])
    for cut in split[1:]:
        gain = gain * one(*cut)
    return gain


def bell_draw(key, dims, spread, bound, pieces=(), kind=jnp.bfloat16):
    drawn = jax.random.normal(key, dims, jnp.float32) * spread
    if len(pieces) > 0:
        drawn = block_levels(key, dims, pieces, -0.22, 0.18) * drawn
    return jnp.clip(drawn, min=-bound, max=bound).astype(kind)


def setup_inputs(seed: int = 0) -> dict:
    key_of = jax.random.split(jax.random.key(seed), 4)
    exposure = jnp.clip(jax.random.uniform(key_of[0], (PATHS, COLS), jnp.float32, -127.0, 127.0) * block_levels(key_of[0], (PATHS, COLS), ((0, 16), (1, 16)), -0.4, 0.0), -127.0, 127.0).astype(jnp.bfloat16)
    scales = draw_scales(jax.random.fold_in(key_of[3], 71), 0)
    sketch = bell_draw(key_of[2], (SKETCH, COLS), COLS ** -0.5, 0.046875, ((1, 16),))
    return dict(exposure=exposure, scales=scales, sketch=sketch)


HIGH = lax.Precision.HIGHEST

def reference(exposure, scales, sketch):
    blocks_a = exposure.reshape(N_PATH, PATH_DEV, BLOCKS, 128)
    blocks_s = scales.reshape(BLOCKS, N_PATH, PATH_DEV).transpose(1, 0, 2)
    sketch3 = sketch.reshape(SKETCH, BLOCKS, 128).astype(jnp.float32)

    def sketch_block(pair):
        codes = pair[0].astype(jnp.float32)
        parts = jnp.einsum('kbc,pbc->bkp', sketch3, codes, precision=HIGH)
        return lax.optimization_barrier(jnp.sum(parts * pair[1][:, None, :], axis=0))
    sketched = lax.map(sketch_block, (blocks_a, blocks_s))
    sketched = sketched.transpose(1, 0, 2).reshape(SKETCH, PATHS)
    gram = jnp.dot(sketched, sketched.T, precision=HIGH)
    factor = jnp.linalg.cholesky(gram)
    orthonormal = lax.linalg.triangular_solve(factor, sketched, left_side=True, lower=True)
    orth_blocks = orthonormal.reshape(SKETCH, N_PATH, PATH_DEV).transpose(1, 0, 2)

    def project(carry, trio):
        weighted = trio[2][None, :, :] * trio[1][:, None, :]
        codes = trio[0].astype(jnp.float32)
        term = jnp.einsum('bkp,pbc->kbc', weighted, codes, precision=HIGH)
        return (carry + term.reshape(SKETCH, COLS), None)
    projected, unused = lax.scan(project, jnp.zeros((SKETCH, COLS), jnp.float32), (blocks_a, blocks_s, orth_blocks))
    basis = orthonormal * jnp.sqrt(jnp.float32(PATHS))
    return (basis, projected)
```

```python
import functools
import jax
import jax.numpy as jnp
from jax import lax
from jax.experimental import pallas as pl
from jax.experimental.pallas import tpu as pltpu
from jax.sharding import PartitionSpec as P

BF = jnp.bfloat16
F32 = jnp.float32
ANY = pl.BlockSpec(memory_space=pl.ANY)
VM = pl.BlockSpec(memory_space=pltpu.VMEM)
LIMIT = 40 * 1024 * 1024
CHUNKS = 4
NT = (((1,), (1,)), ((), ()))


def split2(x):
    hi = x.astype(BF)
    return hi, (x - hi.astype(F32)).astype(BF)


def sketch_kernel(groups, sketch, scales, exposure, out, kept, sems):
    rows, cols = exposure.shape
    blocks = scales.shape[0]
    width = out.shape[2]
    step = rows // CHUNKS
    copies = []
    for c in range(CHUNKS):
        part = pl.ds(c * step, step)
        copies.append(pltpu.make_async_copy(exposure.at[part], kept.at[part], sems.at[c]))
        copies[-1].start()
    for c in range(CHUNKS):
        copies[c].wait()

        @pl.loop(0, step // width)
        def _(i):
            start = pl.multiple_of(c * step + i * width, width)
            span = pl.ds(start, width)
            total = None
            for b in range(blocks):
                lanes = slice(b * 128, (b + 1) * 128)
                term = lax.dot_general(
                    sketch[:, lanes], kept[span, lanes], NT, preferred_element_type=F32
                )
                term = term * scales[b : b + 1, span]
                total = term if total is None else total + term
            out[c * (step // width) + i] = total


def sum_copies_kernel(x, out):
    total = jnp.sum(x[...], axis=0)
    for j in range(out.shape[0]):
        out[j] = total


def add_copies_kernel(a, b, out):
    total = a[...] + b[...]
    for j in range(out.shape[0]):
        out[j] = total


def project_kernel(core, pieces, scales, exposure, mine, other, acc, gram):
    groups, size, width = pieces.shape
    blocks = scales.shape[0]
    acc[...] = jnp.zeros_like(acc)
    gram[...] = jnp.zeros_like(gram)

    @pl.loop(0, groups)
    def _(g):
        span = pl.ds(pl.multiple_of(g * width, width), width)
        s = pieces[g]
        both = jnp.concatenate(split2(s), axis=0)
        gram[...] += lax.dot_general(both, both, NT, preferred_element_type=F32)
        for b in range(blocks):
            lanes = slice(b * 128, (b + 1) * 128)
            w = jnp.concatenate(split2(s * scales[b : b + 1, span]), axis=0)
            acc[:, lanes] += jnp.dot(w, exposure[span, lanes], preferred_element_type=F32)

    half = blocks * 128 // 2
    first = core[0] == 0
    low = acc[:size, :half] + acc[size:, :half]
    high = acc[:size, half:] + acc[size:, half:]
    g = gram[...]
    g = (g[:size, :size] + g[size:, size:]) + (g[:size, size:] + g[size:, :size])
    for ref, part in ((mine, jnp.where(first, low, high)), (other, jnp.where(first, high, low))):
        ref[:, :half] = part
        ref[:, half:] = jnp.zeros_like(ref[:, half:])
        ref[:, half : half + size] = g


def solve_kernel(x, lower, projected):
    size = x.shape[1]
    half = projected.shape[1]
    total = jnp.sum(x[...], axis=0)
    gram = total[:, half : half + size]
    row = lax.broadcasted_iota(jnp.int32, (size, 128), 0)
    lane = lax.broadcasted_iota(jnp.int32, (size, 128), 1)
    eye = jnp.where(lane - size == row, 1.0, 0.0).astype(F32)
    a = jnp.where(lane < size, jnp.pad(gram, ((0, 0), (0, 128 - size))), eye)
    inv = jnp.zeros((size, 128), F32)
    for j in range(size):
        pivot_row = a[j : j + 1, :]
        pivot = pivot_row[:, j : j + 1]
        root = lax.rsqrt(pivot)
        inv = jnp.where(row == j, pivot_row * root, inv)
        if j < size - 1:
            col = a[:, j : j + 1]
            a = a - jnp.where(row > j, (col / pivot) * pivot_row, 0.0)
    linv = inv[:, size : 2 * size]
    lower[...] = linv
    projected[...] = lax.dot_general(
        linv, total[:, :half], (((1,), (0,)), ((), ())),
        precision=lax.Precision.HIGHEST, preferred_element_type=F32,
    )


def basis_kernel(factor, lower, pieces, out):
    groups, size, width = pieces.shape
    hi, lo = split2(lower[...] * factor)
    lhs = jnp.concatenate([hi, lo, hi, lo], axis=1)
    for g in range(groups):
        shi, slo = split2(pieces[g])
        rhs = jnp.concatenate([shi, shi, slo, slo], axis=0)
        out[:, g * width : (g + 1) * width] = jnp.dot(lhs, rhs, preferred_element_type=F32)


def join_kernel(core, mine, other, out):
    half = mine.shape[1]
    first = core[0] == 0
    a, b = mine[...], other[...]
    out[:, :half] = jnp.where(first, a, b)
    out[:, half:] = jnp.where(first, b, a)


def params(**kw):
    return pltpu.CompilerParams(vmem_limit_bytes=LIMIT, **kw)


def per_device(exposure, scales, sketch):
    rows, cols = exposure.shape
    size = sketch.shape[0]
    blocks = scales.shape[0]
    n_col = lax.axis_size(("y", "x"))
    n_z = lax.axis_size("z")
    width = rows // n_col
    half = cols // 2
    wide = half + 128
    total_paths = rows * n_z * lax.axis_size("core")
    core = lax.axis_index("core").astype(jnp.int32).reshape(1)
    SM = pl.BlockSpec(memory_space=pltpu.SMEM)
    shape = jax.ShapeDtypeStruct

    partial, kept = pl.pallas_call(
        functools.partial(sketch_kernel, n_col),
        out_shape=(shape((n_col, size, width), F32), pltpu.VMEM((rows, cols), BF)),
        in_specs=[VM, VM, ANY],
        out_specs=(VM, VM),
        scratch_shapes=[pltpu.SemaphoreType.DMA((CHUNKS,))],
        compiler_params=params(),
        name="sketch",
    )(sketch, scales, exposure)

    got = lax.all_to_all(partial, ("y", "x"), 0, 0)
    spread = pl.pallas_call(
        sum_copies_kernel, out_shape=shape((n_col, size, width), F32),
        in_specs=[VM], out_specs=VM, compiler_params=params(), name="sum_parts",
    )(got)
    pieces = lax.all_to_all(spread, ("y", "x"), 0, 0)

    kept = pltpu.with_memory_space_constraint(kept, pltpu.VMEM)
    mine, other = pl.pallas_call(
        project_kernel,
        out_shape=(shape((size, wide), F32),) * 2,
        in_specs=[SM, VM, VM, VM],
        out_specs=(VM, VM),
        scratch_shapes=[pltpu.VMEM((2 * size, cols), F32), pltpu.VMEM((2 * size, 2 * size), F32)],
        compiler_params=params(),
        name="project",
    )(core, pieces, scales, kept)

    received = lax.ppermute(other, "core", [(0, 1), (1, 0)])
    spread_z = pl.pallas_call(
        add_copies_kernel, out_shape=shape((n_z, size, wide), F32),
        in_specs=[VM, VM], out_specs=VM, compiler_params=params(), name="add_cores",
    )(mine, received)
    got_z = lax.all_to_all(spread_z, "z", 0, 0)

    lower, proj = pl.pallas_call(
        solve_kernel, out_shape=(shape((size, size), F32), shape((size, half), F32)),
        in_specs=[VM], out_specs=(VM, VM), compiler_params=params(), name="solve",
    )(got_z)
    proj_other = lax.ppermute(proj, "core", [(0, 1), (1, 0)])
    basis = pl.pallas_call(
        functools.partial(basis_kernel, float(total_paths) ** 0.5),
        out_shape=shape((size, rows), F32),
        in_specs=[VM, VM], out_specs=VM, compiler_params=params(), name="basis",
    )(lower, pieces)
    projected = pl.pallas_call(
        join_kernel, out_shape=shape((size, cols), F32),
        in_specs=[SM, VM, VM], out_specs=VM, compiler_params=params(), name="join",
    )(core, proj, proj_other)
    return (basis, projected)


def solution(mesh):
    path, col = ("z", "core"), ("y", "x")
    n_path, n_col = mesh.shape["path"], mesh.shape["col"]
    split = jax.sharding.Mesh(mesh.devices.reshape(n_path // 2, 2, 4, n_col // 4), path + col)
    return jax.shard_map(
        per_device,
        mesh=split,
        in_specs=(P(path, col), P(col, path), P(None, col)),
        out_specs=(P(None, path), P(None, col)),
        check_vma=False,
    )
```

```python
import functools
import jax
import jax.numpy as jnp
from jax import lax
from jax.experimental import pallas as pl
from jax.experimental.pallas import tpu as pltpu
from jax.sharding import PartitionSpec as P

BF = jnp.bfloat16
F32 = jnp.float32
ANY = pl.BlockSpec(memory_space=pl.ANY)
VM = pl.BlockSpec(memory_space=pltpu.VMEM)
SM = pl.BlockSpec(memory_space=pltpu.SMEM)
CHUNKS = 4
LANES = 128
NT = (((1,), (1,)), ((), ()))


def split2(x):
    hi = x.astype(BF)
    return hi, (x - hi.astype(F32)).astype(BF)


def lanes(b, n=1):
    return slice(b * LANES, (b + n) * LANES)


def fetch(exposure, held, sems):
    step = held.shape[0] // CHUNKS
    copies = []
    for c in range(CHUNKS):
        part = pl.ds(c * step, step)
        copies.append(pltpu.make_async_copy(exposure.at[part], held.at[part], sems.at[c]))
        copies[-1].start()
    return copies


def sketch_kernel(sketch_hbm, scales_hbm, exposure, out, sketch, scales, held, diag, sems, small):
    size = sketch.shape[0]
    blocks = scales.shape[0]
    groups, _, width = out.shape
    per_chunk = groups // CHUNKS
    first = pltpu.make_async_copy(sketch_hbm, sketch, small.at[0])
    second = pltpu.make_async_copy(scales_hbm, scales, small.at[1])
    first.start()
    second.start()
    copies = fetch(exposure, held, sems)
    diag[...] = jnp.zeros_like(diag)
    first.wait()
    for b in range(blocks):
        diag[b * size : (b + 1) * size, lanes(b)] = sketch[:, lanes(b)]
    second.wait()
    for c in range(CHUNKS):
        copies[c].wait()
        for g in range(c * per_chunk, (c + 1) * per_chunk):
            span = slice(g * width, (g + 1) * width)
            parts = lax.dot_general(diag[...], held[span, :], NT, preferred_element_type=F32)
            total = None
            for b in range(blocks):
                term = parts[b * size : (b + 1) * size] * scales[b : b + 1, span]
                total = term if total is None else total + term
            out[g] = total


def sum_copies_kernel(x, out):
    total = jnp.sum(x[...], axis=0)
    for j in range(out.shape[0]):
        out[j] = total


def add_copies_kernel(a, b, out):
    total = a[...] + b[...]
    for j in range(out.shape[0]):
        out[j] = total


def sum_kernel(x, out):
    out[...] = jnp.sum(x[...], axis=0)


def project_kernel(core, pieces, scales_hbm, exposure, mine, other, scales, held, both, w, acc, sems, small):
    groups, size, width = pieces.shape
    blocks = scales.shape[0]
    per_chunk = groups // CHUNKS
    step = held.shape[0] // CHUNKS
    first = pltpu.make_async_copy(scales_hbm, scales, small.at[0])
    first.start()
    copies = fetch(exposure, held, sems)
    for g in range(groups):
        both[:, g * width : (g + 1) * width] = jnp.concatenate(split2(pieces[g]), axis=0)
    gram = lax.dot_general(both[...], both[...], NT, preferred_element_type=F32)
    gram = (gram[:size, :size] + gram[size:, size:]) + (gram[:size, size:] + gram[size:, :size])
    first.wait()
    for c in range(CHUNKS):
        for g in range(c * per_chunk, (c + 1) * per_chunk):
            span = slice(g * width, (g + 1) * width)
            s = pieces[g]
            for b in range(blocks):
                w[2 * size * b : 2 * size * (b + 1), span] = jnp.concatenate(
                    split2(s * scales[b : b + 1, span]), axis=0
                )
        copies[c].wait()
        rows = slice(c * step, (c + 1) * step)
        for b in range(0, blocks, 2):
            t = jnp.dot(
                w[2 * size * b : 2 * size * (b + 2), rows], held[rows, lanes(b, 2)],
                preferred_element_type=F32,
            )
            t0 = t[:size, :LANES] + t[size : 2 * size, :LANES]
            t1 = t[2 * size : 3 * size, LANES:] + t[3 * size :, LANES:]
            if c == 0:
                acc[b] = t0
                acc[b + 1] = t1
            else:
                acc[b] += t0
                acc[b + 1] += t1

    half = blocks // 2
    is_first = core[0] == 0
    for b in range(half):
        low, high = acc[b], acc[half + b]
        mine[b * size : (b + 1) * size] = jnp.where(is_first, low, high)
        other[b * size : (b + 1) * size] = jnp.where(is_first, high, low)
    rows = LANES // size
    packed = jnp.concatenate([gram[i * size // rows : (i + 1) * size // rows] for i in range(rows)], axis=1)
    mine[half * size :] = packed
    other[half * size :] = packed


def solve_kernel(factor, x, pieces, lower, basis):
    groups, size, width = pieces.shape
    rows = LANES // size
    packed = x[x.shape[0] - size // rows :, :]
    gram = jnp.concatenate([packed[:, i * size : (i + 1) * size] for i in range(rows)], axis=0)
    row = lax.broadcasted_iota(jnp.int32, (size, LANES), 0)
    lane = lax.broadcasted_iota(jnp.int32, (size, LANES), 1)
    eye = jnp.where(lane - size == row, 1.0, 0.0).astype(F32)
    a = jnp.where(lane < size, jnp.pad(gram, ((0, 0), (0, LANES - size))), eye)
    inv = jnp.zeros((size, LANES), F32)
    for j in range(size):
        pivot_row = a[j : j + 1, :]
        pivot = pivot_row[:, j : j + 1]
        inv = jnp.where(row == j, pivot_row * lax.rsqrt(pivot), inv)
        if j < size - 1:
            col = a[:, j : j + 1]
            a = a - jnp.where(row > j, (col / pivot) * pivot_row, 0.0)
    linv = inv[:, size : 2 * size]
    lower[...] = linv
    hi, lo = split2(linv * factor)
    lhs = jnp.concatenate([hi, lo, hi, lo], axis=1)
    for g in range(groups):
        shi, slo = split2(pieces[g])
        rhs = jnp.concatenate([shi, shi, slo, slo], axis=0)
        basis[:, g * width : (g + 1) * width] = jnp.dot(lhs, rhs, preferred_element_type=F32)


def finish_kernel(core, lower, mine, other, out):
    size, cols = out.shape
    half = cols // LANES // 2
    is_first = core[0] == 0
    hi, lo = split2(lower[...])
    lhs = jnp.concatenate([hi, lo, hi, lo], axis=1)
    low, high = [], []
    for b in range(half):
        m, o = mine[b * size : (b + 1) * size], other[b * size : (b + 1) * size]
        low.append(jnp.where(is_first, m, o))
        high.append(jnp.where(is_first, o, m))
    shi, slo = split2(jnp.concatenate(low + high, axis=1))
    rhs = jnp.concatenate([shi, shi, slo, slo], axis=0)
    out[...] = jnp.dot(lhs, rhs, preferred_element_type=F32)


def call(kernel, name, out_shape, in_specs, limit=8, scratch=()):
    single = not isinstance(out_shape, tuple)
    return pl.pallas_call(
        kernel,
        out_shape=out_shape,
        in_specs=in_specs,
        out_specs=VM if single else (VM,) * len(out_shape),
        scratch_shapes=scratch,
        compiler_params=pltpu.CompilerParams(vmem_limit_bytes=limit * 2**20),
        name=name,
    )


def per_device(exposure, scales, sketch):
    rows, cols = exposure.shape
    size = sketch.shape[0]
    blocks = scales.shape[0]
    n_col = lax.axis_size(("y", "x"))
    n_z = lax.axis_size("z")
    width = rows // n_col
    half = blocks // 2 * size
    tall = half + size * size // LANES
    total_paths = rows * n_z * lax.axis_size("core")
    core = lax.axis_index("core").astype(jnp.int32).reshape(1)
    swap = [(0, 1), (1, 0)]
    shape = jax.ShapeDtypeStruct
    DMA = pltpu.SemaphoreType.DMA

    partial = call(
        sketch_kernel, "sketch", shape((n_col, size, width), F32), [ANY] * 3, 40,
        [
            pltpu.VMEM((size, cols), BF), pltpu.VMEM((blocks, rows), F32), pltpu.VMEM((rows, cols), BF),
            pltpu.VMEM((blocks * size, cols), BF), DMA((CHUNKS,)), DMA((2,)),
        ],
    )(sketch, scales, exposure)
    got = lax.all_to_all(partial, ("y", "x"), 0, 0)
    spread = call(sum_copies_kernel, "sum_parts", shape((n_col, size, width), F32), [VM])(got)
    pieces = lax.all_to_all(spread, ("y", "x"), 0, 0)

    mine, other = call(
        project_kernel, "project", (shape((tall, LANES), F32),) * 2, [SM, VM, ANY, ANY], 40,
        [
            pltpu.VMEM((blocks, rows), F32), pltpu.VMEM((rows, cols), BF), pltpu.VMEM((2 * size, rows), BF),
            pltpu.VMEM((2 * size * blocks, rows), BF), pltpu.VMEM((blocks, size, LANES), F32),
            DMA((CHUNKS,)), DMA((1,)),
        ],
    )(core, pieces, scales, exposure)

    received = lax.ppermute(other, "core", swap)
    spread_z = call(add_copies_kernel, "add_cores", shape((n_z, tall, LANES), F32), [VM, VM])(mine, received)
    got_z = lax.all_to_all(spread_z, "z", 0, 0)
    total = call(sum_kernel, "sum_z", shape((tall, LANES), F32), [VM])(got_z)
    total_other = lax.ppermute(total, "core", swap)
    lower, basis = call(
        functools.partial(solve_kernel, float(total_paths) ** 0.5), "solve",
        (shape((size, size), F32), shape((size, rows), F32)), [VM, VM],
    )(total, pieces)
    projected = call(finish_kernel, "finish", shape((size, cols), F32), [SM, VM, VM, VM])(
        core, lower, total, total_other
    )
    return (basis, projected)


def solution(mesh):
    path, col = ("z", "core"), ("y", "x")
    n_path, n_col = mesh.shape["path"], mesh.shape["col"]
    split = jax.sharding.Mesh(mesh.devices.reshape(n_path // 2, 2, 4, n_col // 4), path + col)
    return jax.shard_map(
        per_device,
        mesh=split,
        in_specs=(P(path, col), P(col, path), P(None, col)),
        out_specs=(P(None, path), P(None, col)),
        check_vma=False,
    )
```

```python
import functools
import jax
import jax.numpy as jnp
from jax import lax
from jax.experimental import pallas as pl
from jax.experimental.pallas import tpu as pltpu
from jax.sharding import PartitionSpec as P

BF = jnp.bfloat16
F32 = jnp.float32
HBM = pl.BlockSpec(memory_space=pltpu.HBM)
VM = pl.BlockSpec(memory_space=pltpu.VMEM)
CHUNKS = 4
AHEAD = 2
PANEL = 8
LANES = 128
NT = (((1,), (1,)), ((), ()))


def split2(x):
    hi = x.astype(BF)
    return hi, (x - hi.astype(F32)).astype(BF)


def lanes(b, n=1):
    return slice(b * LANES, (b + n) * LANES)


def sketch_kernel(sketch_hbm, scales_hbm, exposure, out, held, sketch, scales, diag, sems, small):
    size = sketch.shape[0]
    blocks = scales.shape[0]
    groups, _, width = out.shape
    per_chunk = groups // CHUNKS
    first = pltpu.make_async_copy(sketch_hbm, sketch, small.at[0])
    second = pltpu.make_async_copy(scales_hbm, scales, small.at[1])
    first.start()
    second.start()
    step = held.shape[0] // CHUNKS
    copies = []
    for c in range(CHUNKS):
        part = pl.ds(c * step, step)
        copies.append(pltpu.make_async_copy(exposure.at[part], held.at[part], sems.at[c]))
    for copy in copies[:AHEAD]:
        copy.start()
    diag[...] = jnp.zeros_like(diag)
    first.wait()
    for b in range(blocks):
        diag[b * size : (b + 1) * size, lanes(b)] = sketch[:, lanes(b)]
    second.wait()
    for c in range(CHUNKS):
        copies[c].wait()
        if c + AHEAD < CHUNKS:
            copies[c + AHEAD].start()
        for g in range(c * per_chunk, (c + 1) * per_chunk):
            span = slice(g * width, (g + 1) * width)
            parts = lax.dot_general(diag[...], held[span, :], NT, preferred_element_type=F32)
            total = None
            for b in range(blocks):
                term = parts[b * size : (b + 1) * size] * scales[b : b + 1, span]
                total = term if total is None else total + term
            out[g] = total


def sum_copies_kernel(x, out):
    total = jnp.sum(x[...], axis=0)
    for j in range(out.shape[0]):
        out[j] = total


def add_copies_kernel(a, b, out):
    total = a[...] + b[...]
    for j in range(out.shape[0]):
        out[j] = total


def sum_kernel(x, out):
    out[...] = jnp.sum(x[...], axis=0)


def project_kernel(pieces, scales, exposure, mine, other, both, w, acc):
    groups, size, width = pieces.shape
    blocks = scales.shape[0]
    per_chunk = groups // CHUNKS
    step = exposure.shape[0] // CHUNKS
    for g in range(groups):
        both[:, g * width : (g + 1) * width] = jnp.concatenate(split2(pieces[g]), axis=0)
    gram = lax.dot_general(both[...], both[...], NT, preferred_element_type=F32)
    gram = (gram[:size, :size] + gram[size:, size:]) + (gram[:size, size:] + gram[size:, :size])
    for c in range(CHUNKS):
        for g in range(c * per_chunk, (c + 1) * per_chunk):
            span = slice(g * width, (g + 1) * width)
            s = pieces[g]
            for b in range(blocks):
                w[2 * size * b : 2 * size * (b + 1), span] = jnp.concatenate(
                    split2(s * scales[b : b + 1, span]), axis=0
                )
        rows = slice(c * step, (c + 1) * step)
        for b in range(0, blocks, 2):
            t = jnp.dot(
                w[2 * size * b : 2 * size * (b + 2), rows], exposure[rows, lanes(b, 2)],
                preferred_element_type=F32,
            )
            t0 = t[:size, :LANES] + t[size : 2 * size, :LANES]
            t1 = t[2 * size : 3 * size, LANES:] + t[3 * size :, LANES:]
            if c == 0:
                acc[b] = t0
                acc[b + 1] = t1
            else:
                acc[b] += t0
                acc[b + 1] += t1

    half = blocks // 2
    is_first = lax.axis_index("core") == 0
    for b in range(half):
        low, high = acc[b], acc[half + b]
        mine[b * size : (b + 1) * size] = jnp.where(is_first, low, high)
        other[b * size : (b + 1) * size] = jnp.where(is_first, high, low)
    rows = LANES // size
    packed = jnp.concatenate([gram[i * size // rows : (i + 1) * size // rows] for i in range(rows)], axis=1)
    mine[half * size :] = packed
    other[half * size :] = packed


def solve_kernel(factor, x, pieces, lower, basis):
    groups, size, width = pieces.shape
    rows = LANES // size
    packed = x[x.shape[0] - size // rows :, :]
    gram = jnp.concatenate([packed[:, i * size : (i + 1) * size] for i in range(rows)], axis=0)
    row = lax.broadcasted_iota(jnp.int32, (size, LANES), 0)
    lane = lax.broadcasted_iota(jnp.int32, (size, LANES), 1)
    eye = jnp.where(lane - size == row, 1.0, 0.0).astype(F32)
    a = jnp.where(lane < size, jnp.pad(gram, ((0, 0), (0, LANES - size))), eye)
    inv = jnp.zeros((size, LANES), F32)
    for start in range(0, size, PANEL):
        cols = [jnp.broadcast_to(a[:, j : j + 1], (size, LANES)) for j in range(start, start + PANEL)]
        for k in range(PANEL):
            j = start + k
            pivot = cols[k][j : j + 1, :]
            pivot_row = a[j : j + 1, :]
            inv = jnp.where(row == j, pivot_row * lax.rsqrt(pivot), inv)
            scaled = jnp.where(row > j, cols[k] * (1.0 / pivot), 0.0)
            a = a - scaled * pivot_row
            for m in range(k + 1, PANEL):
                cols[m] = cols[m] - scaled * cols[m][j : j + 1, :]
    linv = inv[:, size : 2 * size]
    lower[...] = linv
    hi, lo = split2(linv * factor)
    lhs = jnp.concatenate([hi, lo, hi, lo], axis=1)
    for g in range(groups):
        shi, slo = split2(pieces[g])
        rhs = jnp.concatenate([shi, shi, slo, slo], axis=0)
        basis[:, g * width : (g + 1) * width] = jnp.dot(lhs, rhs, preferred_element_type=F32)


def finish_kernel(lower, mine, other, out):
    size, cols = out.shape
    half = cols // LANES // 2
    is_first = lax.axis_index("core") == 0
    hi, lo = split2(lower[...])
    lhs = jnp.concatenate([hi, lo, hi, lo], axis=1)
    low, high = [], []
    for b in range(half):
        m, o = mine[b * size : (b + 1) * size], other[b * size : (b + 1) * size]
        low.append(jnp.where(is_first, m, o))
        high.append(jnp.where(is_first, o, m))
    shi, slo = split2(jnp.concatenate(low + high, axis=1))
    rhs = jnp.concatenate([shi, shi, slo, slo], axis=0)
    out[...] = jnp.dot(lhs, rhs, preferred_element_type=F32)


def call(kernel, name, out_shape, in_specs, limit=8, scratch=()):
    single = not isinstance(out_shape, tuple)
    return pl.pallas_call(
        kernel,
        out_shape=out_shape,
        in_specs=in_specs,
        out_specs=VM if single else (VM,) * len(out_shape),
        scratch_shapes=scratch,
        compiler_params=pltpu.CompilerParams(vmem_limit_bytes=limit * 2**20),
        name=name,
    )


def per_device(exposure, scales, sketch):
    rows, cols = exposure.shape
    size = sketch.shape[0]
    blocks = scales.shape[0]
    n_col = lax.axis_size(("y", "x"))
    n_z = lax.axis_size("z")
    width = rows // n_col
    half = blocks // 2 * size
    tall = half + size * size // LANES
    total_paths = rows * n_z * lax.axis_size("core")
    swap = [(0, 1), (1, 0)]
    shape = jax.ShapeDtypeStruct
    DMA = pltpu.SemaphoreType.DMA

    partial, held = call(
        sketch_kernel, "sketch", (shape((n_col, size, width), F32), pltpu.VMEM((rows, cols), BF)),
        [HBM] * 3, 40,
        [
            pltpu.VMEM((size, cols), BF), pltpu.VMEM((blocks, rows), F32),
            pltpu.VMEM((blocks * size, cols), BF), DMA((CHUNKS,)), DMA((2,)),
        ],
    )(*(pltpu.with_memory_space_constraint(x, pltpu.HBM) for x in (sketch, scales, exposure)))
    got = lax.all_to_all(partial, ("y", "x"), 0, 0)
    spread = call(sum_copies_kernel, "sum_parts", shape((n_col, size, width), F32), [VM])(got)
    pieces = lax.all_to_all(spread, ("y", "x"), 0, 0)

    mine, other = call(
        project_kernel, "project", (shape((tall, LANES), F32),) * 2, [VM, VM, VM], 40,
        [
            pltpu.VMEM((2 * size, rows), BF), pltpu.VMEM((2 * size * blocks, rows), BF),
            pltpu.VMEM((blocks, size, LANES), F32),
        ],
    )(pieces, scales, held)

    received = lax.ppermute(other, "core", swap)
    spread_z = call(add_copies_kernel, "add_cores", shape((n_z, tall, LANES), F32), [VM, VM])(mine, received)
    got_z = lax.all_to_all(spread_z, "z", 0, 0)
    total = call(sum_kernel, "sum_z", shape((tall, LANES), F32), [VM])(got_z)
    total_other = lax.ppermute(total, "core", swap)
    lower, basis = call(
        functools.partial(solve_kernel, float(total_paths) ** 0.5), "solve",
        (shape((size, size), F32), shape((size, rows), F32)), [VM, VM],
    )(total, pieces)
    projected = call(finish_kernel, "finish", shape((size, cols), F32), [VM, VM, VM])(
        lower, total, total_other
    )
    return (basis, projected)


def solution(mesh):
    path, col = ("z", "core"), ("y", "x")
    n_path, n_col = mesh.shape["path"], mesh.shape["col"]
    split = jax.sharding.Mesh(mesh.devices.reshape(n_path // 2, 2, 4, n_col // 4), path + col)
    return jax.shard_map(
        per_device,
        mesh=split,
        in_specs=(P(path, col), P(col, path), P(None, col)),
        out_specs=(P(None, path), P(None, col)),
        check_vma=False,
    )
```

```python
import functools
import jax
import jax.numpy as jnp
from jax import lax
from jax.experimental import pallas as pl
from jax.experimental.pallas import tpu as pltpu
from jax.sharding import PartitionSpec as P

BF = jnp.bfloat16
F32 = jnp.float32
HBM = pl.BlockSpec(memory_space=pltpu.HBM)
VM = pl.BlockSpec(memory_space=pltpu.VMEM)
CHUNKS = 4
PAIRS = {
    "a": ((0, 1), (2, 3), (4, 5), (6, 7)),
    "b": ((1, 2), (3, 4), (5, 6), (7, 0)),
    "c": ((0, 3), (1, 6), (2, 5), (4, 7)),
}
ORDER = "cba"
AHEAD = 2
PANEL = 8
LANES = 128
NT = (((1,), (1,)), ((), ()))


def split2(x):
    hi = x.astype(BF)
    return hi, (x - hi.astype(F32)).astype(BF)


def lanes(b, n=1):
    return slice(b * LANES, (b + n) * LANES)


def sketch_kernel(sketch_hbm, scales_hbm, exposure, out, held, sketch, scales, diag, sems, small):
    size = sketch.shape[0]
    blocks = scales.shape[0]
    groups, _, width = out.shape
    per_chunk = groups // CHUNKS
    first = pltpu.make_async_copy(sketch_hbm, sketch, small.at[0])
    second = pltpu.make_async_copy(scales_hbm, scales, small.at[1])
    first.start()
    second.start()
    step = held.shape[0] // CHUNKS
    copies = []
    for c in range(CHUNKS):
        part = pl.ds(c * step, step)
        copies.append(pltpu.make_async_copy(exposure.at[part], held.at[part], sems.at[c]))
    for copy in copies[:AHEAD]:
        copy.start()
    diag[...] = jnp.zeros_like(diag)
    first.wait()
    for b in range(blocks):
        diag[b * size : (b + 1) * size, lanes(b)] = sketch[:, lanes(b)]
    second.wait()
    for c in range(CHUNKS):
        copies[c].wait()
        if c + AHEAD < CHUNKS:
            copies[c + AHEAD].start()
        for g in range(c * per_chunk, (c + 1) * per_chunk):
            span = slice(g * width, (g + 1) * width)
            parts = lax.dot_general(diag[...], held[span, :], NT, preferred_element_type=F32)
            total = None
            for b in range(blocks):
                term = parts[b * size : (b + 1) * size] * scales[b : b + 1, span]
                total = term if total is None else total + term
            out[g] = total


def sum_copies_kernel(x, out):
    total = jnp.sum(x[...], axis=0)
    for j in range(out.shape[0]):
        out[j] = total


def add_kernel(a, b, out):
    out[...] = a[...] + b[...]


def project_kernel(pieces, scales, exposure, mine, other, both, w, acc):
    groups, size, width = pieces.shape
    blocks = scales.shape[0]
    per_chunk = groups // CHUNKS
    step = exposure.shape[0] // CHUNKS
    for g in range(groups):
        both[:, g * width : (g + 1) * width] = jnp.concatenate(split2(pieces[g]), axis=0)
    gram = lax.dot_general(both[...], both[...], NT, preferred_element_type=F32)
    gram = (gram[:size, :size] + gram[size:, size:]) + (gram[:size, size:] + gram[size:, :size])
    for c in range(CHUNKS):
        for g in range(c * per_chunk, (c + 1) * per_chunk):
            span = slice(g * width, (g + 1) * width)
            s = pieces[g]
            for b in range(blocks):
                w[2 * size * b : 2 * size * (b + 1), span] = jnp.concatenate(
                    split2(s * scales[b : b + 1, span]), axis=0
                )
        rows = slice(c * step, (c + 1) * step)
        for b in range(0, blocks, 2):
            t = jnp.dot(
                w[2 * size * b : 2 * size * (b + 2), rows], exposure[rows, lanes(b, 2)],
                preferred_element_type=F32,
            )
            t0 = t[:size, :LANES] + t[size : 2 * size, :LANES]
            t1 = t[2 * size : 3 * size, LANES:] + t[3 * size :, LANES:]
            if c == 0:
                acc[b] = t0
                acc[b + 1] = t1
            else:
                acc[b] += t0
                acc[b + 1] += t1

    half = blocks // 2
    is_first = lax.axis_index("core") == 0
    for b in range(half):
        low, high = acc[b], acc[half + b]
        mine[b * size : (b + 1) * size] = jnp.where(is_first, low, high)
        other[b * size : (b + 1) * size] = jnp.where(is_first, high, low)
    rows = LANES // size
    packed = jnp.concatenate([gram[i * size // rows : (i + 1) * size // rows] for i in range(rows)], axis=1)
    mine[half * size :] = packed
    other[half * size :] = packed


def solve_kernel(factor, x, pieces, lower, basis):
    groups, size, width = pieces.shape
    rows = LANES // size
    packed = x[x.shape[0] - size // rows :, :]
    gram = jnp.concatenate([packed[:, i * size : (i + 1) * size] for i in range(rows)], axis=0)
    row = lax.broadcasted_iota(jnp.int32, (size, LANES), 0)
    lane = lax.broadcasted_iota(jnp.int32, (size, LANES), 1)
    eye = jnp.where(lane - size == row, 1.0, 0.0).astype(F32)
    a = jnp.where(lane < size, jnp.pad(gram, ((0, 0), (0, LANES - size))), eye)
    inv = jnp.zeros((size, LANES), F32)
    for start in range(0, size, PANEL):
        cols = [jnp.broadcast_to(a[:, j : j + 1], (size, LANES)) for j in range(start, start + PANEL)]
        for k in range(PANEL):
            j = start + k
            pivot = cols[k][j : j + 1, :]
            pivot_row = a[j : j + 1, :]
            inv = jnp.where(row == j, pivot_row * lax.rsqrt(pivot), inv)
            scaled = jnp.where(row > j, cols[k] * (1.0 / pivot), 0.0)
            a = a - scaled * pivot_row
            for m in range(k + 1, PANEL):
                cols[m] = cols[m] - scaled * cols[m][j : j + 1, :]
    linv = inv[:, size : 2 * size]
    lower[...] = linv
    hi, lo = split2(linv * factor)
    lhs = jnp.concatenate([hi, lo, hi, lo], axis=1)
    for g in range(groups):
        shi, slo = split2(pieces[g])
        rhs = jnp.concatenate([shi, shi, slo, slo], axis=0)
        basis[:, g * width : (g + 1) * width] = jnp.dot(lhs, rhs, preferred_element_type=F32)


def finish_kernel(lower, mine, other, out):
    size, cols = out.shape
    half = cols // LANES // 2
    is_first = lax.axis_index("core") == 0
    hi, lo = split2(lower[...])
    lhs = jnp.concatenate([hi, lo, hi, lo], axis=1)
    low, high = [], []
    for b in range(half):
        m, o = mine[b * size : (b + 1) * size], other[b * size : (b + 1) * size]
        low.append(jnp.where(is_first, m, o))
        high.append(jnp.where(is_first, o, m))
    shi, slo = split2(jnp.concatenate(low + high, axis=1))
    rhs = jnp.concatenate([shi, shi, slo, slo], axis=0)
    out[...] = jnp.dot(lhs, rhs, preferred_element_type=F32)


def call(kernel, name, out_shape, in_specs, limit=8, scratch=()):
    single = not isinstance(out_shape, tuple)
    return pl.pallas_call(
        kernel,
        out_shape=out_shape,
        in_specs=in_specs,
        out_specs=VM if single else (VM,) * len(out_shape),
        scratch_shapes=scratch,
        compiler_params=pltpu.CompilerParams(vmem_limit_bytes=limit * 2**20),
        name=name,
    )


def per_device(exposure, scales, sketch):
    rows, cols = exposure.shape
    size = sketch.shape[0]
    blocks = scales.shape[0]
    n_col = lax.axis_size(("y", "x"))
    n_z = lax.axis_size("z")
    width = rows // n_col
    half = blocks // 2 * size
    tall = half + size * size // LANES
    total_paths = rows * n_z * lax.axis_size("core")
    swap = [(0, 1), (1, 0)]
    shape = jax.ShapeDtypeStruct
    DMA = pltpu.SemaphoreType.DMA

    partial, held = call(
        sketch_kernel, "sketch", (shape((n_col, size, width), F32), pltpu.VMEM((rows, cols), BF)),
        [HBM] * 3, 40,
        [
            pltpu.VMEM((size, cols), BF), pltpu.VMEM((blocks, rows), F32),
            pltpu.VMEM((blocks * size, cols), BF), DMA((CHUNKS,)), DMA((2,)),
        ],
    )(*(pltpu.with_memory_space_constraint(x, pltpu.HBM) for x in (sketch, scales, exposure)))
    got = lax.all_to_all(partial, ("y", "x"), 0, 0)
    spread = call(sum_copies_kernel, "sum_parts", shape((n_col, size, width), F32), [VM])(got)
    pieces = lax.all_to_all(spread, ("y", "x"), 0, 0)

    mine, other = call(
        project_kernel, "project", (shape((tall, LANES), F32),) * 2, [VM, VM, VM], 40,
        [
            pltpu.VMEM((2 * size, rows), BF), pltpu.VMEM((2 * size * blocks, rows), BF),
            pltpu.VMEM((blocks, size, LANES), F32),
        ],
    )(pieces, scales, held)

    add = call(add_kernel, "add", shape((tall, LANES), F32), [VM, VM])
    total = add(mine, lax.ppermute(other, "core", swap))
    for step in ORDER:
        both_ways = [p for i, j in PAIRS[step] for p in ((i, j), (j, i))]
        total = add(total, lax.ppermute(total, "z", both_ways))
    total_other = lax.ppermute(total, "core", swap)
    lower, basis = call(
        functools.partial(solve_kernel, float(total_paths) ** 0.5), "solve",
        (shape((size, size), F32), shape((size, rows), F32)), [VM, VM],
    )(total, pieces)
    projected = call(finish_kernel, "finish", shape((size, cols), F32), [VM, VM, VM])(
        lower, total, total_other
    )
    return (basis, projected)


def solution(mesh):
    path, col = ("z", "core"), ("y", "x")
    n_path, n_col = mesh.shape["path"], mesh.shape["col"]
    split = jax.sharding.Mesh(mesh.devices.reshape(n_path // 2, 2, 4, n_col // 4), path + col)
    return jax.shard_map(
        per_device,
        mesh=split,
        in_specs=(P(path, col), P(col, path), P(None, col)),
        out_specs=(P(None, path), P(None, col)),
        check_vma=False,
    )
```

```python
import functools
import jax
import jax.numpy as jnp
from jax import lax
from jax.experimental import pallas as pl
from jax.experimental.pallas import tpu as pltpu
from jax.sharding import PartitionSpec as P

BF = jnp.bfloat16
F32 = jnp.float32
HBM = pl.BlockSpec(memory_space=pltpu.HBM)
VM = pl.BlockSpec(memory_space=pltpu.VMEM)
CHUNKS = 4
AHEAD = 2
PANEL = 8
LANES = 128
NT = (((1,), (1,)), ((), ()))


def split2(x):
    hi = x.astype(BF)
    return hi, (x - hi.astype(F32)).astype(BF)


def lanes(b, n=1):
    return slice(b * LANES, (b + n) * LANES)


def sketch_kernel(sketch_hbm, scales_hbm, exposure, out, held, sketch, scales, diag, sems, small):
    size = sketch.shape[0]
    blocks = scales.shape[0]
    groups, _, width = out.shape
    per_chunk = groups // CHUNKS
    first = pltpu.make_async_copy(sketch_hbm, sketch, small.at[0])
    second = pltpu.make_async_copy(scales_hbm, scales, small.at[1])
    first.start()
    second.start()
    step = held.shape[0] // CHUNKS
    copies = []
    for c in range(CHUNKS):
        part = pl.ds(c * step, step)
        copies.append(pltpu.make_async_copy(exposure.at[part], held.at[part], sems.at[c]))
    for copy in copies[:AHEAD]:
        copy.start()
    diag[...] = jnp.zeros_like(diag)
    first.wait()
    for b in range(blocks):
        diag[b * size : (b + 1) * size, lanes(b)] = sketch[:, lanes(b)]
    second.wait()
    for c in range(CHUNKS):
        copies[c].wait()
        if c + AHEAD < CHUNKS:
            copies[c + AHEAD].start()
        for g in range(c * per_chunk, (c + 1) * per_chunk):
            span = slice(g * width, (g + 1) * width)
            parts = lax.dot_general(diag[...], held[span, :], NT, preferred_element_type=F32)
            total = None
            for b in range(blocks):
                term = parts[b * size : (b + 1) * size] * scales[b : b + 1, span]
                total = term if total is None else total + term
            out[g] = total


def sum_copies_kernel(x, out):
    total = jnp.sum(x[...], axis=0)
    for j in range(out.shape[0]):
        out[j] = total


def add_kernel(a, b, out):
    out[...] = a[...] + b[...]


def add_four_kernel(a, b, c, d, out):
    out[...] = (a[...] + b[...]) + (c[...] + d[...])


def project_kernel(pieces, scales, exposure, mine, other, both, w, acc):
    groups, size, width = pieces.shape
    blocks = scales.shape[0]
    per_chunk = groups // CHUNKS
    step = exposure.shape[0] // CHUNKS
    for g in range(groups):
        both[:, g * width : (g + 1) * width] = jnp.concatenate(split2(pieces[g]), axis=0)
    gram = lax.dot_general(both[...], both[...], NT, preferred_element_type=F32)
    gram = (gram[:size, :size] + gram[size:, size:]) + (gram[:size, size:] + gram[size:, :size])
    for c in range(CHUNKS):
        for g in range(c * per_chunk, (c + 1) * per_chunk):
            span = slice(g * width, (g + 1) * width)
            s = pieces[g]
            for b in range(blocks):
                w[2 * size * b : 2 * size * (b + 1), span] = jnp.concatenate(
                    split2(s * scales[b : b + 1, span]), axis=0
                )
        rows = slice(c * step, (c + 1) * step)
        for b in range(0, blocks, 2):
            t = jnp.dot(
                w[2 * size * b : 2 * size * (b + 2), rows], exposure[rows, lanes(b, 2)],
                preferred_element_type=F32,
            )
            t0 = t[:size, :LANES] + t[size : 2 * size, :LANES]
            t1 = t[2 * size : 3 * size, LANES:] + t[3 * size :, LANES:]
            if c == 0:
                acc[b] = t0
                acc[b + 1] = t1
            else:
                acc[b] += t0
                acc[b + 1] += t1

    half = blocks // 2
    is_first = lax.axis_index("core") == 0
    for b in range(half):
        low, high = acc[b], acc[half + b]
        mine[b * size : (b + 1) * size] = jnp.where(is_first, low, high)
        other[b * size : (b + 1) * size] = jnp.where(is_first, high, low)
    rows = LANES // size
    packed = jnp.concatenate([gram[i * size // rows : (i + 1) * size // rows] for i in range(rows)], axis=1)
    mine[half * size :] = packed
    other[half * size :] = packed


def solve_kernel(factor, mine, across, beside, corner, pieces, basis, projected):
    groups, size, width = pieces.shape
    rows = LANES // size
    x = mine[...] + across[...]
    y = beside[...] + corner[...]
    packed = x[x.shape[0] - size // rows :, :]
    gram = jnp.concatenate([packed[:, i * size : (i + 1) * size] for i in range(rows)], axis=0)
    row = lax.broadcasted_iota(jnp.int32, (size, LANES), 0)
    lane = lax.broadcasted_iota(jnp.int32, (size, LANES), 1)
    eye = jnp.where(lane - size == row, 1.0, 0.0).astype(F32)
    a = jnp.where(lane < size, jnp.pad(gram, ((0, 0), (0, LANES - size))), eye)
    inv = jnp.zeros((size, LANES), F32)
    for start in range(0, size, PANEL):
        cols = [jnp.broadcast_to(a[:, j : j + 1], (size, LANES)) for j in range(start, start + PANEL)]
        for k in range(PANEL):
            j = start + k
            pivot = cols[k][j : j + 1, :]
            pivot_row = a[j : j + 1, :]
            inv = jnp.where(row == j, pivot_row * lax.rsqrt(pivot), inv)
            scaled = jnp.where(row > j, cols[k] * (1.0 / pivot), 0.0)
            a = a - scaled * pivot_row
            for m in range(k + 1, PANEL):
                cols[m] = cols[m] - scaled * cols[m][j : j + 1, :]
    linv = inv[:, size : 2 * size]
    lhs = jnp.concatenate(split2(linv) * 2, axis=1)
    half = projected.shape[1] // LANES // 2
    is_first = lax.axis_index("core") == 0
    low = jnp.concatenate([x[b * size : (b + 1) * size] for b in range(half)], axis=1)
    high = jnp.concatenate([y[b * size : (b + 1) * size] for b in range(half)], axis=1)
    low, high = jnp.where(is_first, low, high), jnp.where(is_first, high, low)
    for part, at in ((low, 0), (high, half * LANES)):
        shi, slo = split2(part)
        rhs = jnp.concatenate([shi, shi, slo, slo], axis=0)
        projected[:, at : at + half * LANES] = jnp.dot(lhs, rhs, preferred_element_type=F32)
    lhs = jnp.concatenate(split2(linv * factor) * 2, axis=1)
    for g in range(groups):
        shi, slo = split2(pieces[g])
        rhs = jnp.concatenate([shi, shi, slo, slo], axis=0)
        basis[:, g * width : (g + 1) * width] = jnp.dot(lhs, rhs, preferred_element_type=F32)


def call(kernel, name, out_shape, in_specs, limit=8, scratch=()):
    single = not isinstance(out_shape, tuple)
    return pl.pallas_call(
        kernel,
        out_shape=out_shape,
        in_specs=in_specs,
        out_specs=VM if single else (VM,) * len(out_shape),
        scratch_shapes=scratch,
        compiler_params=pltpu.CompilerParams(vmem_limit_bytes=limit * 2**20),
        name=name,
    )


def per_device(exposure, scales, sketch):
    rows, cols = exposure.shape
    size = sketch.shape[0]
    blocks = scales.shape[0]
    n_col = lax.axis_size(("y", "x"))
    n_z = lax.axis_size("z")
    width = rows // n_col
    half = blocks // 2 * size
    tall = half + size * size // LANES
    total_paths = rows * n_z * lax.axis_size("core")
    swap = [(0, 1), (1, 0)]
    shape = jax.ShapeDtypeStruct
    DMA = pltpu.SemaphoreType.DMA

    partial, held = call(
        sketch_kernel, "sketch", (shape((n_col, size, width), F32), pltpu.VMEM((rows, cols), BF)),
        [HBM] * 3, 40,
        [
            pltpu.VMEM((size, cols), BF), pltpu.VMEM((blocks, rows), F32),
            pltpu.VMEM((blocks * size, cols), BF), DMA((CHUNKS,)), DMA((2,)),
        ],
    )(*(pltpu.with_memory_space_constraint(x, pltpu.HBM) for x in (sketch, scales, exposure)))
    got = lax.all_to_all(partial, ("y", "x"), 0, 0)
    spread = call(sum_copies_kernel, "sum_parts", shape((n_col, size, width), F32), [VM])(got)
    pieces = lax.all_to_all(spread, ("y", "x"), 0, 0)

    mine, other = call(
        project_kernel, "project", (shape((tall, LANES), F32),) * 2, [VM, VM, VM], 40,
        [
            pltpu.VMEM((2 * size, rows), BF), pltpu.VMEM((2 * size * blocks, rows), BF),
            pltpu.VMEM((blocks, size, LANES), F32),
        ],
    )(pieces, scales, held)

    def add(*xs):
        kernel = add_kernel if len(xs) == 2 else add_four_kernel
        return call(kernel, "add", shape((tall, LANES), F32), [VM] * len(xs))(*xs)

    def swapped(x, swaps):
        return lax.ppermute(x, "z", [p for i, j in swaps for p in ((i, j), (j, i))])

    total = add(mine, lax.ppermute(other, "core", swap))
    total = add(total, swapped(total, ((0, 3), (1, 6), (2, 5), (4, 7))))
    total = add(total, swapped(total, ((1, 2), (3, 4), (5, 6), (7, 0))))
    links = [p for i, j in ((0, 1), (2, 3), (4, 5), (6, 7)) for p in ((i, j), (j, i))]
    across = lax.ppermute(total, "z", links)
    beside = lax.ppermute(total, "core", swap)
    corner = lax.ppermute(
        total, ("z", "core"), [(2 * i + c, 2 * j + 1 - c) for i, j in links for c in range(2)]
    )
    basis, projected = call(
        functools.partial(solve_kernel, float(total_paths) ** 0.5), "solve",
        (shape((size, rows), F32), shape((size, cols), F32)), [VM] * 5,
    )(total, across, beside, corner, pieces)
    return (basis, projected)


def solution(mesh):
    path, col = ("z", "core"), ("y", "x")
    n_path, n_col = mesh.shape["path"], mesh.shape["col"]
    split = jax.sharding.Mesh(mesh.devices.reshape(n_path // 2, 2, 4, n_col // 4), path + col)
    return jax.shard_map(
        per_device,
        mesh=split,
        in_specs=(P(path, col), P(col, path), P(None, col)),
        out_specs=(P(None, path), P(None, col)),
        check_vma=False,
    )
```

```python
import functools
import jax
import jax.numpy as jnp
from jax import lax
from jax.experimental import pallas as pl
from jax.experimental.pallas import tpu as pltpu
from jax.sharding import PartitionSpec as P

BF = jnp.bfloat16
F32 = jnp.float32
HBM = pl.BlockSpec(memory_space=pltpu.HBM)
VM = pl.BlockSpec(memory_space=pltpu.VMEM)
CHUNKS = 4
AHEAD = 2
PANEL = 16
LANES = 128
NT = (((1,), (1,)), ((), ()))


def split2(x):
    hi = x.astype(BF)
    return hi, (x - hi.astype(F32)).astype(BF)


def lanes(b, n=1):
    return slice(b * LANES, (b + n) * LANES)


def sketch_kernel(sketch_hbm, scales_hbm, exposure, out, held, scales, sketch, diag, sems, small):
    size = sketch.shape[0]
    blocks = scales.shape[0]
    groups, _, width = out.shape
    per_chunk = groups // CHUNKS
    first = pltpu.make_async_copy(sketch_hbm, sketch, small.at[0])
    second = pltpu.make_async_copy(scales_hbm, scales, small.at[1])
    first.start()
    second.start()
    step = held.shape[0] // CHUNKS
    copies = []
    for c in range(CHUNKS):
        part = pl.ds(c * step, step)
        copies.append(pltpu.make_async_copy(exposure.at[part], held.at[part], sems.at[c]))
    for copy in copies[:AHEAD]:
        copy.start()
    diag[...] = jnp.zeros_like(diag)
    first.wait()
    for b in range(blocks):
        diag[b * size : (b + 1) * size, lanes(b)] = sketch[:, lanes(b)]
    second.wait()
    for c in range(CHUNKS):
        copies[c].wait()
        if c + AHEAD < CHUNKS:
            copies[c + AHEAD].start()
        for g in range(c * per_chunk, (c + 1) * per_chunk):
            span = slice(g * width, (g + 1) * width)
            parts = lax.dot_general(diag[...], held[span, :], NT, preferred_element_type=F32)
            total = None
            for b in range(blocks):
                term = parts[b * size : (b + 1) * size] * scales[b : b + 1, span]
                total = term if total is None else total + term
            out[g] = total


def sum_copies_kernel(x, out):
    total = jnp.sum(x[...], axis=0)
    for j in range(out.shape[0]):
        out[j] = total


def add_kernel(a, b, out):
    out[...] = a[...] + b[...]


def add_four_kernel(a, b, c, d, out):
    out[...] = (a[...] + b[...]) + (c[...] + d[...])


def project_kernel(pieces, scales, exposure, mine, other, both, w, acc):
    groups, size, width = pieces.shape
    blocks = scales.shape[0]
    per_chunk = groups // CHUNKS
    step = exposure.shape[0] // CHUNKS
    for g in range(groups):
        both[:, g * width : (g + 1) * width] = jnp.concatenate(split2(pieces[g]), axis=0)
    gram = lax.dot_general(both[...], both[...], NT, preferred_element_type=F32)
    gram = (gram[:size, :size] + gram[size:, size:]) + (gram[:size, size:] + gram[size:, :size])
    for c in range(CHUNKS):
        for g in range(c * per_chunk, (c + 1) * per_chunk):
            span = slice(g * width, (g + 1) * width)
            s = pieces[g]
            for b in range(blocks):
                w[2 * size * b : 2 * size * (b + 1), span] = jnp.concatenate(
                    split2(s * scales[b : b + 1, span]), axis=0
                )
        rows = slice(c * step, (c + 1) * step)
        for b in range(0, blocks, 2):
            t = jnp.dot(
                w[2 * size * b : 2 * size * (b + 2), rows], exposure[rows, lanes(b, 2)],
                preferred_element_type=F32,
            )
            t0 = t[:size, :LANES] + t[size : 2 * size, :LANES]
            t1 = t[2 * size : 3 * size, LANES:] + t[3 * size :, LANES:]
            if c == 0:
                acc[b] = t0
                acc[b + 1] = t1
            else:
                acc[b] += t0
                acc[b + 1] += t1

    half = blocks // 2
    is_first = lax.axis_index("core") == 0
    for b in range(half):
        low, high = acc[b], acc[half + b]
        mine[b * size : (b + 1) * size] = jnp.where(is_first, low, high)
        other[b * size : (b + 1) * size] = jnp.where(is_first, high, low)
    rows = LANES // size
    packed = jnp.concatenate([gram[i * size // rows : (i + 1) * size // rows] for i in range(rows)], axis=1)
    mine[half * size :] = packed
    other[half * size :] = packed


def solve_kernel(factor, mine, across, beside, corner, pieces, basis, projected):
    groups, size, width = pieces.shape
    rows = LANES // size
    x = mine[...] + across[...]
    y = beside[...] + corner[...]
    packed = x[x.shape[0] - size // rows :, :]
    gram = jnp.concatenate([packed[:, i * size : (i + 1) * size] for i in range(rows)], axis=0)
    row = lax.broadcasted_iota(jnp.int32, (size, LANES), 0)
    lane = lax.broadcasted_iota(jnp.int32, (size, LANES), 1)
    eye = jnp.where(lane - size == row, 1.0, 0.0).astype(F32)
    a = jnp.where(lane < size, jnp.pad(gram, ((0, 0), (0, LANES - size))), eye)
    inv = jnp.zeros((size, LANES), F32)
    for start in range(0, size, PANEL):
        cols = [jnp.broadcast_to(a[:, j : j + 1], (size, LANES)) for j in range(start, start + PANEL)]
        for k in range(PANEL):
            j = start + k
            pivot = cols[k][j : j + 1, :]
            pivot_row = a[j : j + 1, :]
            inv = jnp.where(row == j, pivot_row * lax.rsqrt(pivot), inv)
            scaled = jnp.where(row > j, cols[k] * (1.0 / pivot), 0.0)
            a = a - scaled * pivot_row
            for m in range(k + 1, PANEL):
                cols[m] = cols[m] - scaled * cols[m][j : j + 1, :]
    linv = inv[:, size : 2 * size]
    lhs = jnp.concatenate(split2(linv) * 2, axis=1)
    half = projected.shape[1] // LANES // 2
    is_first = lax.axis_index("core") == 0
    low = jnp.concatenate([x[b * size : (b + 1) * size] for b in range(half)], axis=1)
    high = jnp.concatenate([y[b * size : (b + 1) * size] for b in range(half)], axis=1)
    low, high = jnp.where(is_first, low, high), jnp.where(is_first, high, low)
    for part, at in ((low, 0), (high, half * LANES)):
        shi, slo = split2(part)
        rhs = jnp.concatenate([shi, shi, slo, slo], axis=0)
        projected[:, at : at + half * LANES] = jnp.dot(lhs, rhs, preferred_element_type=F32)
    lhs = jnp.concatenate(split2(linv * factor) * 2, axis=1)
    for g in range(groups):
        shi, slo = split2(pieces[g])
        rhs = jnp.concatenate([shi, shi, slo, slo], axis=0)
        basis[:, g * width : (g + 1) * width] = jnp.dot(lhs, rhs, preferred_element_type=F32)


def call(kernel, name, out_shape, in_specs, limit=8, scratch=()):
    single = not isinstance(out_shape, tuple)
    return pl.pallas_call(
        kernel,
        out_shape=out_shape,
        in_specs=in_specs,
        out_specs=VM if single else (VM,) * len(out_shape),
        scratch_shapes=scratch,
        compiler_params=pltpu.CompilerParams(vmem_limit_bytes=limit * 2**20),
        name=name,
    )


def per_device(exposure, scales, sketch):
    rows, cols = exposure.shape
    size = sketch.shape[0]
    blocks = scales.shape[0]
    n_col = lax.axis_size(("y", "x"))
    n_z = lax.axis_size("z")
    width = rows // n_col
    half = blocks // 2 * size
    tall = half + size * size // LANES
    total_paths = rows * n_z * lax.axis_size("core")
    swap = [(0, 1), (1, 0)]
    shape = jax.ShapeDtypeStruct
    DMA = pltpu.SemaphoreType.DMA

    partial, held, scales = call(
        sketch_kernel, "sketch",
        (shape((n_col, size, width), F32), pltpu.VMEM((rows, cols), BF), pltpu.VMEM((blocks, rows), F32)),
        [HBM] * 3, 40,
        [
            pltpu.VMEM((size, cols), BF),
            pltpu.VMEM((blocks * size, cols), BF), DMA((CHUNKS,)), DMA((2,)),
        ],
    )(*(pltpu.with_memory_space_constraint(x, pltpu.HBM) for x in (sketch, scales, exposure)))
    got = lax.all_to_all(partial, ("x", "y"), 0, 0)
    spread = call(sum_copies_kernel, "sum_parts", shape((n_col, size, width), F32), [VM])(got)
    pieces = lax.all_to_all(spread, ("x", "y"), 0, 0)

    mine, other = call(
        project_kernel, "project", (shape((tall, LANES), F32),) * 2, [VM, VM, VM], 40,
        [
            pltpu.VMEM((2 * size, rows), BF), pltpu.VMEM((2 * size * blocks, rows), BF),
            pltpu.VMEM((blocks, size, LANES), F32),
        ],
    )(pieces, scales, held)

    def add(*xs):
        kernel = add_kernel if len(xs) == 2 else add_four_kernel
        return call(kernel, "add", shape((tall, LANES), F32), [VM] * len(xs))(*xs)

    def swapped(x, swaps):
        return lax.ppermute(x, "z", [p for i, j in swaps for p in ((i, j), (j, i))])

    total = add(mine, lax.ppermute(other, "core", swap))
    total = add(total, swapped(total, ((0, 3), (1, 6), (2, 5), (4, 7))))
    total = add(total, swapped(total, ((1, 2), (3, 4), (5, 6), (7, 0))))
    links = [p for i, j in ((0, 1), (2, 3), (4, 5), (6, 7)) for p in ((i, j), (j, i))]
    across = lax.ppermute(total, "z", links)
    beside = lax.ppermute(total, "core", swap)
    corner = lax.ppermute(
        total, ("z", "core"), [(2 * i + c, 2 * j + 1 - c) for i, j in links for c in range(2)]
    )
    basis, projected = call(
        functools.partial(solve_kernel, float(total_paths) ** 0.5), "solve",
        (shape((size, rows), F32), shape((size, cols), F32)), [VM] * 5,
    )(total, across, beside, corner, pieces)
    return (basis, projected)


def solution(mesh):
    path, col = ("z", "core"), ("y", "x")
    n_path, n_col = mesh.shape["path"], mesh.shape["col"]
    split = jax.sharding.Mesh(mesh.devices.reshape(n_path // 2, 2, 4, n_col // 4), path + col)
    return jax.shard_map(
        per_device,
        mesh=split,
        in_specs=(P(path, col), P(col, path), P(None, col)),
        out_specs=(P(None, path), P(None, col)),
        check_vma=False,
    )
```

```python
import functools
import jax
import jax.numpy as jnp
from jax import lax
from jax.experimental import pallas as pl
from jax.experimental.pallas import tpu as pltpu
from jax.sharding import PartitionSpec as P

BF = jnp.bfloat16
F32 = jnp.float32
HBM = pl.BlockSpec(memory_space=pltpu.HBM)
VM = pl.BlockSpec(memory_space=pltpu.VMEM)
CHUNKS = 4
AHEAD = 2
PANEL = 16
LANES = 128
GROUPS = [[4 * (j % 4) + j // 4 for j in range(16)], [31 - j for j in range(16)]]
NT = (((1,), (1,)), ((), ()))


def split2(x):
    hi = x.astype(BF)
    return hi, (x - hi.astype(F32)).astype(BF)


def lanes(b, n=1):
    return slice(b * LANES, (b + n) * LANES)


def sketch_kernel(sketch_hbm, scales_hbm, exposure, out, held, scales, sketch, diag, sems, small):
    size = sketch.shape[0]
    blocks = scales.shape[0]
    groups, _, width = out.shape
    per_chunk = groups // CHUNKS
    first = pltpu.make_async_copy(sketch_hbm, sketch, small.at[0])
    second = pltpu.make_async_copy(scales_hbm, scales, small.at[1])
    first.start()
    second.start()
    step = held.shape[0] // CHUNKS
    copies = []
    for c in range(CHUNKS):
        part = pl.ds(c * step, step)
        copies.append(pltpu.make_async_copy(exposure.at[part], held.at[part], sems.at[c]))
    for copy in copies[:AHEAD]:
        copy.start()
    diag[...] = jnp.zeros_like(diag)
    first.wait()
    for b in range(blocks):
        diag[b * size : (b + 1) * size, lanes(b)] = sketch[:, lanes(b)]
    second.wait()
    for c in range(CHUNKS):
        copies[c].wait()
        if c + AHEAD < CHUNKS:
            copies[c + AHEAD].start()
        for g in range(c * per_chunk, (c + 1) * per_chunk):
            span = slice(g * width, (g + 1) * width)
            parts = lax.dot_general(diag[...], held[span, :], NT, preferred_element_type=F32)
            total = None
            for b in range(blocks):
                term = parts[b * size : (b + 1) * size] * scales[b : b + 1, span]
                total = term if total is None else total + term
            out[g] = total


def sum_copies_kernel(x, out):
    total = jnp.sum(x[...], axis=0)
    for j in range(out.shape[0]):
        out[j] = total


def add_kernel(a, b, out):
    out[...] = a[...] + b[...]


def add_four_kernel(a, b, c, d, out):
    out[...] = (a[...] + b[...]) + (c[...] + d[...])


def project_kernel(pieces, scales, exposure, mine, other, both, w, acc):
    groups, size, width = pieces.shape
    blocks = scales.shape[0]
    per_chunk = groups // CHUNKS
    step = exposure.shape[0] // CHUNKS
    for g in range(groups):
        both[:, g * width : (g + 1) * width] = jnp.concatenate(split2(pieces[g]), axis=0)
    gram = lax.dot_general(both[...], both[...], NT, preferred_element_type=F32)
    gram = (gram[:size, :size] + gram[size:, size:]) + (gram[:size, size:] + gram[size:, :size])
    for c in range(CHUNKS):
        for g in range(c * per_chunk, (c + 1) * per_chunk):
            span = slice(g * width, (g + 1) * width)
            s = pieces[g]
            for b in range(blocks):
                w[2 * size * b : 2 * size * (b + 1), span] = jnp.concatenate(
                    split2(s * scales[b : b + 1, span]), axis=0
                )
        rows = slice(c * step, (c + 1) * step)
        for b in range(0, blocks, 2):
            t = jnp.dot(
                w[2 * size * b : 2 * size * (b + 2), rows], exposure[rows, lanes(b, 2)],
                preferred_element_type=F32,
            )
            t0 = t[:size, :LANES] + t[size : 2 * size, :LANES]
            t1 = t[2 * size : 3 * size, LANES:] + t[3 * size :, LANES:]
            if c == 0:
                acc[b] = t0
                acc[b + 1] = t1
            else:
                acc[b] += t0
                acc[b + 1] += t1

    half = blocks // 2
    is_first = lax.axis_index("core") == 0
    for b in range(half):
        low, high = acc[b], acc[half + b]
        mine[b * size : (b + 1) * size] = jnp.where(is_first, low, high)
        other[b * size : (b + 1) * size] = jnp.where(is_first, high, low)
    rows = LANES // size
    packed = jnp.concatenate([gram[i * size // rows : (i + 1) * size // rows] for i in range(rows)], axis=1)
    mine[half * size :] = packed
    other[half * size :] = packed


def solve_kernel(factor, mine, across, beside, corner, pieces, basis, projected):
    groups, size, width = pieces.shape
    rows = LANES // size
    x = mine[...] + across[...]
    y = beside[...] + corner[...]
    packed = x[x.shape[0] - size // rows :, :]
    gram = jnp.concatenate([packed[:, i * size : (i + 1) * size] for i in range(rows)], axis=0)
    row = lax.broadcasted_iota(jnp.int32, (size, LANES), 0)
    lane = lax.broadcasted_iota(jnp.int32, (size, LANES), 1)
    eye = jnp.where(lane - size == row, 1.0, 0.0).astype(F32)
    a = jnp.where(lane < size, jnp.pad(gram, ((0, 0), (0, LANES - size))), eye)
    inv = jnp.zeros((size, LANES), F32)
    for start in range(0, size, PANEL):
        cols = [jnp.broadcast_to(a[:, j : j + 1], (size, LANES)) for j in range(start, start + PANEL)]
        for k in range(PANEL):
            j = start + k
            pivot = cols[k][j : j + 1, :]
            pivot_row = a[j : j + 1, :]
            inv = jnp.where(row == j, pivot_row * lax.rsqrt(pivot), inv)
            scaled = jnp.where(row > j, cols[k] * (1.0 / pivot), 0.0)
            a = a - scaled * pivot_row
            for m in range(k + 1, PANEL):
                cols[m] = cols[m] - scaled * cols[m][j : j + 1, :]
    linv = inv[:, size : 2 * size]
    lhs = jnp.concatenate(split2(linv) * 2, axis=1)
    half = projected.shape[1] // LANES // 2
    is_first = lax.axis_index("core") == 0
    low = jnp.concatenate([x[b * size : (b + 1) * size] for b in range(half)], axis=1)
    high = jnp.concatenate([y[b * size : (b + 1) * size] for b in range(half)], axis=1)
    low, high = jnp.where(is_first, low, high), jnp.where(is_first, high, low)
    for part, at in ((low, 0), (high, half * LANES)):
        shi, slo = split2(part)
        rhs = jnp.concatenate([shi, shi, slo, slo], axis=0)
        projected[:, at : at + half * LANES] = jnp.dot(lhs, rhs, preferred_element_type=F32)
    lhs = jnp.concatenate(split2(linv * factor) * 2, axis=1)
    for g in range(groups):
        shi, slo = split2(pieces[g])
        rhs = jnp.concatenate([shi, shi, slo, slo], axis=0)
        basis[:, g * width : (g + 1) * width] = jnp.dot(lhs, rhs, preferred_element_type=F32)


def call(kernel, name, out_shape, in_specs, limit=8, scratch=()):
    single = not isinstance(out_shape, tuple)
    return pl.pallas_call(
        kernel,
        out_shape=out_shape,
        in_specs=in_specs,
        out_specs=VM if single else (VM,) * len(out_shape),
        scratch_shapes=scratch,
        compiler_params=pltpu.CompilerParams(vmem_limit_bytes=limit * 2**20),
        name=name,
    )


def per_device(exposure, scales, sketch):
    rows, cols = exposure.shape
    size = sketch.shape[0]
    blocks = scales.shape[0]
    n_col = lax.axis_size(("y", "x"))
    n_z = lax.axis_size("z")
    width = rows // n_col
    half = blocks // 2 * size
    tall = half + size * size // LANES
    total_paths = rows * n_z * lax.axis_size("core")
    swap = [(0, 1), (1, 0)]
    shape = jax.ShapeDtypeStruct
    DMA = pltpu.SemaphoreType.DMA

    partial, held, scales = call(
        sketch_kernel, "sketch",
        (shape((n_col, size, width), F32), pltpu.VMEM((rows, cols), BF), pltpu.VMEM((blocks, rows), F32)),
        [HBM] * 3, 40,
        [
            pltpu.VMEM((size, cols), BF),
            pltpu.VMEM((blocks * size, cols), BF), DMA((CHUNKS,)), DMA((2,)),
        ],
    )(*(pltpu.with_memory_space_constraint(x, pltpu.HBM) for x in (sketch, scales, exposure)))
    got = lax.all_to_all(partial, ("core", "y", "x"), 0, 0, axis_index_groups=GROUPS)
    spread = call(sum_copies_kernel, "sum_parts", shape((n_col, size, width), F32), [VM])(got)
    pieces = lax.all_to_all(spread, ("core", "y", "x"), 0, 0, axis_index_groups=GROUPS)

    mine, other = call(
        project_kernel, "project", (shape((tall, LANES), F32),) * 2, [VM, VM, VM], 40,
        [
            pltpu.VMEM((2 * size, rows), BF), pltpu.VMEM((2 * size * blocks, rows), BF),
            pltpu.VMEM((blocks, size, LANES), F32),
        ],
    )(pieces, scales, held)

    def add(*xs):
        kernel = add_kernel if len(xs) == 2 else add_four_kernel
        return call(kernel, "add", shape((tall, LANES), F32), [VM] * len(xs))(*xs)

    def swapped(x, swaps):
        return lax.ppermute(x, "z", [p for i, j in swaps for p in ((i, j), (j, i))])

    total = add(mine, lax.ppermute(other, "core", swap))
    total = add(total, swapped(total, ((0, 3), (1, 6), (2, 5), (4, 7))))
    total = add(total, swapped(total, ((1, 2), (3, 4), (5, 6), (7, 0))))
    links = [p for i, j in ((0, 1), (2, 3), (4, 5), (6, 7)) for p in ((i, j), (j, i))]
    across = lax.ppermute(total, "z", links)
    beside = lax.ppermute(total, "core", swap)
    corner = lax.ppermute(
        total, ("z", "core"), [(2 * i + c, 2 * j + 1 - c) for i, j in links for c in range(2)]
    )
    basis, projected = call(
        functools.partial(solve_kernel, float(total_paths) ** 0.5), "solve",
        (shape((size, rows), F32), shape((size, cols), F32)), [VM] * 5,
    )(total, across, beside, corner, pieces)
    return (basis, projected)


def solution(mesh):
    path, col = ("z", "core"), ("y", "x")
    n_path, n_col = mesh.shape["path"], mesh.shape["col"]
    split = jax.sharding.Mesh(mesh.devices.reshape(n_path // 2, 2, 4, n_col // 4), path + col)
    return jax.shard_map(
        per_device,
        mesh=split,
        in_specs=(P(path, col), P(col, path), P(None, col)),
        out_specs=(P(None, path), P(None, col)),
        check_vma=False,
    )
```

```python
import functools
import jax
import jax.numpy as jnp
from jax import lax
from jax.experimental import pallas as pl
from jax.experimental.pallas import tpu as pltpu
from jax.sharding import PartitionSpec as P

BF = jnp.bfloat16
F32 = jnp.float32
HBM = pl.BlockSpec(memory_space=pltpu.HBM)
VM = pl.BlockSpec(memory_space=pltpu.VMEM)
CHUNKS = 4
AHEAD = 2
PANEL = 16
LANES = 128
GROUPS = [
    [4 * (j % 4) + j // 4 for j in range(16)],
    [16 + 4 * ((j + j // 4) % 4) + j % 4 for j in reversed(range(16))],
]
NT = (((1,), (1,)), ((), ()))


def split2(x):
    hi = x.astype(BF)
    return hi, (x - hi.astype(F32)).astype(BF)


def lanes(b, n=1):
    return slice(b * LANES, (b + n) * LANES)


def sketch_kernel(sketch_hbm, scales_hbm, exposure, out, held, scales, sketch, diag, sems, small):
    size = sketch.shape[0]
    blocks = scales.shape[0]
    groups, _, width = out.shape
    per_chunk = groups // CHUNKS
    first = pltpu.make_async_copy(sketch_hbm, sketch, small.at[0])
    second = pltpu.make_async_copy(scales_hbm, scales, small.at[1])
    first.start()
    second.start()
    step = held.shape[0] // CHUNKS
    copies = []
    for c in range(CHUNKS):
        part = pl.ds(c * step, step)
        copies.append(pltpu.make_async_copy(exposure.at[part], held.at[part], sems.at[c]))
    for copy in copies[:AHEAD]:
        copy.start()
    diag[...] = jnp.zeros_like(diag)
    first.wait()
    for b in range(blocks):
        diag[b * size : (b + 1) * size, lanes(b)] = sketch[:, lanes(b)]
    second.wait()
    for c in range(CHUNKS):
        copies[c].wait()
        if c + AHEAD < CHUNKS:
            copies[c + AHEAD].start()
        for g in range(c * per_chunk, (c + 1) * per_chunk):
            span = slice(g * width, (g + 1) * width)
            parts = lax.dot_general(diag[...], held[span, :], NT, preferred_element_type=F32)
            total = None
            for b in range(blocks):
                term = parts[b * size : (b + 1) * size] * scales[b : b + 1, span]
                total = term if total is None else total + term
            out[g] = total


def sum_copies_kernel(x, out):
    total = jnp.sum(x[...], axis=0)
    for j in range(out.shape[0]):
        out[j] = total


def add_kernel(a, b, out):
    out[...] = a[...] + b[...]


def add_four_kernel(a, b, c, d, out):
    out[...] = (a[...] + b[...]) + (c[...] + d[...])


def project_kernel(pieces, scales, exposure, mine, other, both, w, acc):
    groups, size, width = pieces.shape
    blocks = scales.shape[0]
    per_chunk = groups // CHUNKS
    step = exposure.shape[0] // CHUNKS
    for g in range(groups):
        both[:, g * width : (g + 1) * width] = jnp.concatenate(split2(pieces[g]), axis=0)
    gram = lax.dot_general(both[...], both[...], NT, preferred_element_type=F32)
    gram = (gram[:size, :size] + gram[size:, size:]) + (gram[:size, size:] + gram[size:, :size])
    for c in range(CHUNKS):
        for g in range(c * per_chunk, (c + 1) * per_chunk):
            span = slice(g * width, (g + 1) * width)
            s = pieces[g]
            for b in range(blocks):
                w[2 * size * b : 2 * size * (b + 1), span] = jnp.concatenate(
                    split2(s * scales[b : b + 1, span]), axis=0
                )
        rows = slice(c * step, (c + 1) * step)
        for b in range(0, blocks, 2):
            t = jnp.dot(
                w[2 * size * b : 2 * size * (b + 2), rows], exposure[rows, lanes(b, 2)],
                preferred_element_type=F32,
            )
            t0 = t[:size, :LANES] + t[size : 2 * size, :LANES]
            t1 = t[2 * size : 3 * size, LANES:] + t[3 * size :, LANES:]
            if c == 0:
                acc[b] = t0
                acc[b + 1] = t1
            else:
                acc[b] += t0
                acc[b + 1] += t1

    half = blocks // 2
    is_first = lax.axis_index("core") == 0
    for b in range(half):
        low, high = acc[b], acc[half + b]
        mine[b * size : (b + 1) * size] = jnp.where(is_first, low, high)
        other[b * size : (b + 1) * size] = jnp.where(is_first, high, low)
    rows = LANES // size
    packed = jnp.concatenate([gram[i * size // rows : (i + 1) * size // rows] for i in range(rows)], axis=1)
    mine[half * size :] = packed
    other[half * size :] = packed


def solve_kernel(factor, mine, across, beside, corner, pieces, basis, projected):
    groups, size, width = pieces.shape
    rows = LANES // size
    x = mine[...] + across[...]
    y = beside[...] + corner[...]
    packed = x[x.shape[0] - size // rows :, :]
    gram = jnp.concatenate([packed[:, i * size : (i + 1) * size] for i in range(rows)], axis=0)
    row = lax.broadcasted_iota(jnp.int32, (size, LANES), 0)
    lane = lax.broadcasted_iota(jnp.int32, (size, LANES), 1)
    eye = jnp.where(lane - size == row, 1.0, 0.0).astype(F32)
    a = jnp.where(lane < size, jnp.pad(gram, ((0, 0), (0, LANES - size))), eye)
    inv = jnp.zeros((size, LANES), F32)
    for start in range(0, size, PANEL):
        cols = [jnp.broadcast_to(a[:, j : j + 1], (size, LANES)) for j in range(start, start + PANEL)]
        for k in range(PANEL):
            j = start + k
            pivot = cols[k][j : j + 1, :]
            pivot_row = a[j : j + 1, :]
            inv = jnp.where(row == j, pivot_row * lax.rsqrt(pivot), inv)
            scaled = jnp.where(row > j, cols[k] * (1.0 / pivot), 0.0)
            a = a - scaled * pivot_row
            for m in range(k + 1, PANEL):
                cols[m] = cols[m] - scaled * cols[m][j : j + 1, :]
    linv = inv[:, size : 2 * size]
    lhs = jnp.concatenate(split2(linv) * 2, axis=1)
    half = projected.shape[1] // LANES // 2
    is_first = lax.axis_index("core") == 0
    low = jnp.concatenate([x[b * size : (b + 1) * size] for b in range(half)], axis=1)
    high = jnp.concatenate([y[b * size : (b + 1) * size] for b in range(half)], axis=1)
    low, high = jnp.where(is_first, low, high), jnp.where(is_first, high, low)
    for part, at in ((low, 0), (high, half * LANES)):
        shi, slo = split2(part)
        rhs = jnp.concatenate([shi, shi, slo, slo], axis=0)
        projected[:, at : at + half * LANES] = jnp.dot(lhs, rhs, preferred_element_type=F32)
    lhs = jnp.concatenate(split2(linv * factor) * 2, axis=1)
    for g in range(groups):
        shi, slo = split2(pieces[g])
        rhs = jnp.concatenate([shi, shi, slo, slo], axis=0)
        basis[:, g * width : (g + 1) * width] = jnp.dot(lhs, rhs, preferred_element_type=F32)


def call(kernel, name, out_shape, in_specs, limit=8, scratch=()):
    single = not isinstance(out_shape, tuple)
    return pl.pallas_call(
        kernel,
        out_shape=out_shape,
        in_specs=in_specs,
        out_specs=VM if single else (VM,) * len(out_shape),
        scratch_shapes=scratch,
        compiler_params=pltpu.CompilerParams(vmem_limit_bytes=limit * 2**20),
        name=name,
    )


def per_device(exposure, scales, sketch):
    rows, cols = exposure.shape
    size = sketch.shape[0]
    blocks = scales.shape[0]
    n_col = lax.axis_size(("y", "x"))
    n_z = lax.axis_size("z")
    width = rows // n_col
    half = blocks // 2 * size
    tall = half + size * size // LANES
    total_paths = rows * n_z * lax.axis_size("core")
    swap = [(0, 1), (1, 0)]
    shape = jax.ShapeDtypeStruct
    DMA = pltpu.SemaphoreType.DMA

    partial, held, scales = call(
        sketch_kernel, "sketch",
        (shape((n_col, size, width), F32), pltpu.VMEM((rows, cols), BF), pltpu.VMEM((blocks, rows), F32)),
        [HBM] * 3, 40,
        [
            pltpu.VMEM((size, cols), BF),
            pltpu.VMEM((blocks * size, cols), BF), DMA((CHUNKS,)), DMA((2,)),
        ],
    )(*(pltpu.with_memory_space_constraint(x, pltpu.HBM) for x in (sketch, scales, exposure)))
    got = lax.all_to_all(partial, ("core", "y", "x"), 0, 0, axis_index_groups=GROUPS)
    spread = call(sum_copies_kernel, "sum_parts", shape((n_col, size, width), F32), [VM])(got)
    pieces = lax.all_to_all(spread, ("core", "y", "x"), 0, 0, axis_index_groups=GROUPS)

    mine, other = call(
        project_kernel, "project", (shape((tall, LANES), F32),) * 2, [VM, VM, VM], 40,
        [
            pltpu.VMEM((2 * size, rows), BF), pltpu.VMEM((2 * size * blocks, rows), BF),
            pltpu.VMEM((blocks, size, LANES), F32),
        ],
    )(pieces, scales, held)

    def add(*xs):
        kernel = add_kernel if len(xs) == 2 else add_four_kernel
        return call(kernel, "add", shape((tall, LANES), F32), [VM] * len(xs))(*xs)

    def swapped(x, swaps):
        return lax.ppermute(x, "z", [p for i, j in swaps for p in ((i, j), (j, i))])

    total = add(mine, lax.ppermute(other, "core", swap))
    total = add(total, swapped(total, ((0, 3), (1, 6), (2, 5), (4, 7))))
    total = add(total, swapped(total, ((1, 2), (3, 4), (5, 6), (7, 0))))
    links = [p for i, j in ((0, 1), (2, 3), (4, 5), (6, 7)) for p in ((i, j), (j, i))]
    across = lax.ppermute(total, "z", links)
    beside = lax.ppermute(total, "core", swap)
    corner = lax.ppermute(
        total, ("z", "core"), [(2 * i + c, 2 * j + 1 - c) for i, j in links for c in range(2)]
    )
    basis, projected = call(
        functools.partial(solve_kernel, float(total_paths) ** 0.5), "solve",
        (shape((size, rows), F32), shape((size, cols), F32)), [VM] * 5,
    )(total, across, beside, corner, pieces)
    return (basis, projected)


def solution(mesh):
    path, col = ("z", "core"), ("y", "x")
    n_path, n_col = mesh.shape["path"], mesh.shape["col"]
    split = jax.sharding.Mesh(mesh.devices.reshape(n_path // 2, 2, 4, n_col // 4), path + col)
    return jax.shard_map(
        per_device,
        mesh=split,
        in_specs=(P(path, col), P(col, path), P(None, col)),
        out_specs=(P(None, path), P(None, col)),
        check_vma=False,
    )
```

```python
import functools
import jax
import jax.numpy as jnp
from jax import lax
from jax.experimental import pallas as pl
from jax.experimental.pallas import tpu as pltpu
from jax.sharding import PartitionSpec as P

BF = jnp.bfloat16
F32 = jnp.float32
HBM = pl.BlockSpec(memory_space=pltpu.HBM)
VM = pl.BlockSpec(memory_space=pltpu.VMEM)
CHUNKS = 4
PAIRS = {
    "a": ((0, 1), (2, 3), (4, 5), (6, 7)),
    "b": ((1, 2), (3, 4), (5, 6), (7, 0)),
    "c": ((0, 3), (1, 6), (2, 5), (4, 7)),
}
ORDER = "cba"
AHEAD = 2
PANEL = 16
LANES = 128
GROUPS = [
    [4 * (j % 4) + j // 4 for j in range(16)],
    [16 + 4 * ((j + j // 4) % 4) + j % 4 for j in reversed(range(16))],
]
NT = (((1,), (1,)), ((), ()))


def split2(x):
    hi = x.astype(BF)
    return hi, (x - hi.astype(F32)).astype(BF)


def lanes(b, n=1):
    return slice(b * LANES, (b + n) * LANES)


def sketch_kernel(sketch_hbm, scales_hbm, exposure, out, held, scales, sketch, diag, sems, small):
    size = sketch.shape[0]
    blocks = scales.shape[0]
    groups, _, width = out.shape
    per_chunk = groups // CHUNKS
    first = pltpu.make_async_copy(sketch_hbm, sketch, small.at[0])
    second = pltpu.make_async_copy(scales_hbm, scales, small.at[1])
    first.start()
    second.start()
    step = held.shape[0] // CHUNKS
    copies = []
    for c in range(CHUNKS):
        part = pl.ds(c * step, step)
        copies.append(pltpu.make_async_copy(exposure.at[part], held.at[part], sems.at[c]))
    for copy in copies[:AHEAD]:
        copy.start()
    diag[...] = jnp.zeros_like(diag)
    first.wait()
    for b in range(blocks):
        diag[b * size : (b + 1) * size, lanes(b)] = sketch[:, lanes(b)]
    second.wait()
    for c in range(CHUNKS):
        copies[c].wait()
        if c + AHEAD < CHUNKS:
            copies[c + AHEAD].start()
        for g in range(c * per_chunk, (c + 1) * per_chunk):
            span = slice(g * width, (g + 1) * width)
            parts = lax.dot_general(diag[...], held[span, :], NT, preferred_element_type=F32)
            total = None
            for b in range(blocks):
                term = parts[b * size : (b + 1) * size] * scales[b : b + 1, span]
                total = term if total is None else total + term
            out[g] = total


def sum_copies_kernel(x, out):
    total = jnp.sum(x[...], axis=0)
    for j in range(out.shape[0]):
        out[j] = total


def add_kernel(*refs):
    parts = [r[...] for r in refs[:-1]]
    while len(parts) > 1:
        parts = [parts[i] + parts[i + 1] for i in range(0, len(parts), 2)]
    refs[-1][...] = parts[0]


def project_kernel(pieces, scales, exposure, mine, other, both, w, acc):
    groups, size, width = pieces.shape
    blocks = scales.shape[0]
    per_chunk = groups // CHUNKS
    step = exposure.shape[0] // CHUNKS
    for g in range(groups):
        both[:, g * width : (g + 1) * width] = jnp.concatenate(split2(pieces[g]), axis=0)
    gram = lax.dot_general(both[...], both[...], NT, preferred_element_type=F32)
    gram = (gram[:size, :size] + gram[size:, size:]) + (gram[:size, size:] + gram[size:, :size])
    for c in range(CHUNKS):
        for g in range(c * per_chunk, (c + 1) * per_chunk):
            span = slice(g * width, (g + 1) * width)
            s = pieces[g]
            for b in range(blocks):
                w[2 * size * b : 2 * size * (b + 1), span] = jnp.concatenate(
                    split2(s * scales[b : b + 1, span]), axis=0
                )
        rows = slice(c * step, (c + 1) * step)
        for b in range(0, blocks, 2):
            t = jnp.dot(
                w[2 * size * b : 2 * size * (b + 2), rows], exposure[rows, lanes(b, 2)],
                preferred_element_type=F32,
            )
            t0 = t[:size, :LANES] + t[size : 2 * size, :LANES]
            t1 = t[2 * size : 3 * size, LANES:] + t[3 * size :, LANES:]
            if c == 0:
                acc[b] = t0
                acc[b + 1] = t1
            else:
                acc[b] += t0
                acc[b + 1] += t1

    half = blocks // 2
    is_first = lax.axis_index("core") == 0
    for b in range(half):
        low, high = acc[b], acc[half + b]
        mine[b * size : (b + 1) * size] = jnp.where(is_first, low, high)
        other[b * size : (b + 1) * size] = jnp.where(is_first, high, low)
    rows = LANES // size
    packed = jnp.concatenate([gram[i * size // rows : (i + 1) * size // rows] for i in range(rows)], axis=1)
    mine[half * size :] = packed
    other[half * size :] = packed


def solve_kernel(factor, x, pieces, lower, basis):
    groups, size, width = pieces.shape
    rows = LANES // size
    packed = x[x.shape[0] - size // rows :, :]
    gram = jnp.concatenate([packed[:, i * size : (i + 1) * size] for i in range(rows)], axis=0)
    row = lax.broadcasted_iota(jnp.int32, (size, LANES), 0)
    lane = lax.broadcasted_iota(jnp.int32, (size, LANES), 1)
    eye = jnp.where(lane - size == row, 1.0, 0.0).astype(F32)
    a = jnp.where(lane < size, jnp.pad(gram, ((0, 0), (0, LANES - size))), eye)
    inv = jnp.zeros((size, LANES), F32)
    for start in range(0, size, PANEL):
        cols = [jnp.broadcast_to(a[:, j : j + 1], (size, LANES)) for j in range(start, start + PANEL)]
        for k in range(PANEL):
            j = start + k
            pivot = cols[k][j : j + 1, :]
            pivot_row = a[j : j + 1, :]
            inv = jnp.where(row == j, pivot_row * lax.rsqrt(pivot), inv)
            scaled = jnp.where(row > j, cols[k] * (1.0 / pivot), 0.0)
            a = a - scaled * pivot_row
            for m in range(k + 1, PANEL):
                cols[m] = cols[m] - scaled * cols[m][j : j + 1, :]
    linv = inv[:, size : 2 * size]
    lower[...] = linv
    hi, lo = split2(linv * factor)
    lhs = jnp.concatenate([hi, lo, hi, lo], axis=1)
    for g in range(groups):
        shi, slo = split2(pieces[g])
        rhs = jnp.concatenate([shi, shi, slo, slo], axis=0)
        basis[:, g * width : (g + 1) * width] = jnp.dot(lhs, rhs, preferred_element_type=F32)


def finish_kernel(lower, mine, other, out):
    size, cols = out.shape
    half = cols // LANES // 2
    is_first = lax.axis_index("core") == 0
    hi, lo = split2(lower[...])
    lhs = jnp.concatenate([hi, lo, hi, lo], axis=1)
    low, high = [], []
    for b in range(half):
        m, o = mine[b * size : (b + 1) * size], other[b * size : (b + 1) * size]
        low.append(jnp.where(is_first, m, o))
        high.append(jnp.where(is_first, o, m))
    shi, slo = split2(jnp.concatenate(low + high, axis=1))
    rhs = jnp.concatenate([shi, shi, slo, slo], axis=0)
    out[...] = jnp.dot(lhs, rhs, preferred_element_type=F32)


def call(kernel, name, out_shape, in_specs, limit=8, scratch=()):
    single = not isinstance(out_shape, tuple)
    return pl.pallas_call(
        kernel,
        out_shape=out_shape,
        in_specs=in_specs,
        out_specs=VM if single else (VM,) * len(out_shape),
        scratch_shapes=scratch,
        compiler_params=pltpu.CompilerParams(vmem_limit_bytes=limit * 2**20),
        name=name,
    )


def per_device(exposure, scales, sketch):
    rows, cols = exposure.shape
    size = sketch.shape[0]
    blocks = scales.shape[0]
    n_col = lax.axis_size(("y", "x"))
    n_z = lax.axis_size("z")
    width = rows // n_col
    half = blocks // 2 * size
    tall = half + size * size // LANES
    total_paths = rows * n_z * lax.axis_size("core")
    swap = [(0, 1), (1, 0)]
    shape = jax.ShapeDtypeStruct
    DMA = pltpu.SemaphoreType.DMA

    partial, held, scales = call(
        sketch_kernel, "sketch",
        (shape((n_col, size, width), F32), pltpu.VMEM((rows, cols), BF), pltpu.VMEM((blocks, rows), F32)),
        [HBM] * 3, 40,
        [
            pltpu.VMEM((size, cols), BF),
            pltpu.VMEM((blocks * size, cols), BF), DMA((CHUNKS,)), DMA((2,)),
        ],
    )(*(pltpu.with_memory_space_constraint(x, pltpu.HBM) for x in (sketch, scales, exposure)))
    got = lax.all_to_all(partial, ("core", "y", "x"), 0, 0, axis_index_groups=GROUPS)
    spread = call(sum_copies_kernel, "sum_parts", shape((n_col, size, width), F32), [VM])(got)
    pieces = lax.all_to_all(spread, ("core", "y", "x"), 0, 0, axis_index_groups=GROUPS)

    mine, other = call(
        project_kernel, "project", (shape((tall, LANES), F32),) * 2, [VM, VM, VM], 40,
        [
            pltpu.VMEM((2 * size, rows), BF), pltpu.VMEM((2 * size * blocks, rows), BF),
            pltpu.VMEM((blocks, size, LANES), F32),
        ],
    )(pieces, scales, held)

    def add(*xs):
        return call(add_kernel, "add", shape((tall, LANES), F32), [VM] * len(xs))(*xs)

    def pairs(x, swaps):
        return add(x, lax.ppermute(x, "z", [p for i, j in swaps for p in ((i, j), (j, i))]))

    def quad(x, moves):
        return add(x, *(lax.ppermute(x, "z", [(i, f(i)) for i in range(n_z)]) for f in moves))

    total = add(mine, lax.ppermute(other, "core", swap))
    total = pairs(total, ((0, 1), (2, 3), (4, 5), (6, 7)))
    total = add(
        total, lax.ppermute(total, "z", [p for i, j in ((0, 3), (1, 2), (4, 7), (5, 6)) for p in ((i, j), (j, i))]),
        lax.ppermute(total, "z", [p for i, j in ((0, 7), (3, 4), (1, 6), (2, 5)) for p in ((i, j), (j, i))]),
        lax.ppermute(total, "z", [p for i, j in ((0, 5), (1, 4), (2, 7), (3, 6)) for p in ((i, j), (j, i))]),
    )
    total_other = lax.ppermute(total, "core", swap)
    lower, basis = call(
        functools.partial(solve_kernel, float(total_paths) ** 0.5), "solve",
        (shape((size, size), F32), shape((size, rows), F32)), [VM, VM],
    )(total, pieces)
    projected = call(finish_kernel, "finish", shape((size, cols), F32), [VM, VM, VM])(
        lower, total, total_other
    )
    return (basis, projected)


def solution(mesh):
    path, col = ("z", "core"), ("y", "x")
    n_path, n_col = mesh.shape["path"], mesh.shape["col"]
    split = jax.sharding.Mesh(mesh.devices.reshape(n_path // 2, 2, 4, n_col // 4), path + col)
    return jax.shard_map(
        per_device,
        mesh=split,
        in_specs=(P(path, col), P(col, path), P(None, col)),
        out_specs=(P(None, path), P(None, col)),
        check_vma=False,
    )
```
